768 devices in a mesh: dp: 16 (over z_lo, x), rows: 48 (over z_hi, y, core).
Axes of the slice: x: 4, y: 8, z: 12 (z_hi: 3, z_lo: 4; z = z_hi * 4 + z_lo), core: 2. Of those that a mesh axis runs over, the one named last changes fastest.
Arguments:
- images: float32 [196608, 1152], P(('dp', 'rows')), may hold values from -0.2 to 0.2
- texts: float32 [196608, 1152], P(('dp', 'rows')), may hold values from -0.2 to 0.2
- log_temp: float32 [1], replicated, may hold values from 0.7 to 1.8
- bias: float32 [1], replicated, may hold values from -3 to -1
Outputs:
- row_loss: float32 [196608], P(('dp', 'rows'))
- image_grad: float32 [196608, 1152], P(('dp', 'rows'))
- text_grad: float32 [196608, 1152], P(('dp', 'rows'))
The draws below stay inside these ranges and needn't reach their ends.
All inputs are finite; a program needn't handle non-finite values.
Results may differ from the reference program's by a relative error of at most 0.0091.
Values may be sent and summed in bfloat16 or wider, within the bound.
No kernel may reach another device: no remote copies, remote signals or barrier semaphores. Data moves between devices by JAX's collectives and lax.ppermute only.
A program may use at most 32 MiB of HBM per device.

```python
import jax
import jax.numpy as jnp
from jax import lax

D = 1152
ROWS_DEV = 256
STEPS = 4
BLOCKS = 768
PAIRS = 196608


def level_of(stream_key, shape, split, smallest, largest):
    loudness = 1.0
    for position, shards_of in split:
        draws = jax.random.uniform(jax.random.fold_in(jax.random.fold_in(stream_key, 6), position), (shards_of,), jnp.float32, smallest / len(split), largest / len(split))
        loudness = loudness * jnp.repeat(jnp.exp(draws), shape[position] // shards_of).reshape((-1,) + (1,) * (len(shape) - 1 - position))
    return loudness


def bell_draw(stream_key, extent, deviation, bound, split=(), kind=jnp.bfloat16):
    drawn = jax.random.normal(stream_key, extent, jnp.float32) * deviation
    if len(split) > 0:
        drawn = level_of(stream_key, extent, split, -0.22, 0.18) * drawn
    return jnp.clip(drawn, min=-bound, max=bound).astype(kind)


def setup_inputs(seed: int = 0) -> dict:
    streams_of = jax.random.split(jax.random.key(seed), 5)
    images = bell_draw(streams_of[0], (PAIRS, D), (1.0 / 32), 0.2, ((0, 768),), jnp.float32)
    texts = bell_draw(streams_of[1], (PAIRS, D), (1.0 / 32), 0.2, ((0, 768),), jnp.float32)
    log_temp = jnp.clip(jax.random.uniform(streams_of[2], (1,), jnp.float32, 0.7, 1.8), 0.7, 1.8)
    bias = jnp.clip(jax.random.uniform(streams_of[3], (1,), jnp.float32, -3.0, -1.0), -3.0, -1.0)
    return dict(images=images, texts=texts, log_temp=log_temp, bias=bias)


def unit_rows(values):
    norms = jnp.sqrt(lax.optimization_barrier(jnp.sum(values * values, axis=-1, keepdims=True)) + 1e-06)
    return (values / norms, norms)

def back_rows(unit, norms, grad_unit):
    along = lax.optimization_barrier(jnp.sum(unit * grad_unit, axis=-1, keepdims=True))
    return (grad_unit - unit * along) / norms

def reference(images, texts, log_temp, bias):
    scale = jnp.exp(log_temp[0])
    shift_b = bias[0]
    img_unit, img_norm = unit_rows(images)
    txt_unit, txt_norm = unit_rows(texts)
    img_half = img_unit.astype(jnp.bfloat16).reshape(BLOCKS, ROWS_DEV, D)
    txt_half = txt_unit.astype(jnp.bfloat16).reshape(BLOCKS, ROWS_DEV, D)
    img_wide = img_half.astype(jnp.float32)
    eye = jnp.eye(ROWS_DEV, dtype=jnp.float32)
    loss_sum = jnp.zeros((BLOCKS, ROWS_DEV), jnp.float32)
    img_grad_unit = jnp.zeros((BLOCKS, ROWS_DEV, D), jnp.float32)
    txt_grad_unit = jnp.zeros((BLOCKS, ROWS_DEV, D), jnp.float32)
    for step in range(STEPS):
        visit = jnp.roll(txt_half, step, axis=0).astype(jnp.float32)
        logits = scale * jnp.einsum('bik,bjk->bij', img_wide, visit) + shift_b
        if step == 0:
            sign = 2.0 * eye - 1.0
        else:
            sign = -jnp.ones_like(eye)
        loss_sum = loss_sum + lax.optimization_barrier(jnp.sum(jax.nn.softplus(-sign * logits), axis=-1))
        dlogit = (-sign * jax.nn.sigmoid(-sign * logits) * scale).astype(jnp.bfloat16).astype(jnp.float32)
        img_grad_unit = img_grad_unit + jnp.einsum('bij,bjk->bik', dlogit, visit)
        part = jnp.einsum('bij,bik->bjk', dlogit, img_wide)
        txt_grad_unit = txt_grad_unit + jnp.roll(part, -step, axis=0)
    row_loss = (loss_sum / (STEPS * ROWS_DEV)).reshape(PAIRS)
    image_grad = back_rows(img_unit, img_norm, img_grad_unit.reshape(PAIRS, D))
    text_grad = back_rows(txt_unit, txt_norm, txt_grad_unit.reshape(PAIRS, D))
    return (row_loss, image_grad, text_grad)
```

```python
import jax
import jax.numpy as jnp
from jax import lax
from jax.sharding import PartitionSpec as P

BAND = 4
AXES = ("dp", "rows")
X, Y, Z, CORES = 4, 8, 12, 2
COUNT = X * Y * Z * CORES
Z_LO, Z_HI = 4, 3


def place(k):
    core = k % CORES
    y = (k // CORES) % Y
    z_hi = (k // (CORES * Y)) % Z_HI
    x = (k // (CORES * Y * Z_HI)) % X
    z_lo = k // (CORES * Y * Z_HI * X)
    return x, y, z_hi * Z_LO + z_lo, core


INDEX = {place(k): k for k in range(COUNT)}


def routes():
    up, down, far, turn_near, turn_far, swap = [], [], [], [], [], []
    for k in range(COUNT):
        x, y, z, core = place(k)
        swap.append((k, k ^ 1))
        if core == 1 and y == Y - 1:
            stop = INDEX[(x, 0, z, 1)]
            up.append((k, stop))
            turn_near.append((stop, (k + 2) % COUNT))
            stop = INDEX[(x, 1, z, 0)]
            far.append((k, stop))
            turn_far.append((stop, (k + 3) % COUNT))
        else:
            up.append((k, (k + 2) % COUNT))
            if core == 1:
                far.append((k, (k + 3) % COUNT))
        if core == 0 and y == 0:
            stop = INDEX[(x, Y - 1, z, 0)]
            down.append((k, stop))
            turn_near.append((stop, (k - 2) % COUNT))
            stop = INDEX[(x, Y - 2, z, 1)]
            far.append((k, stop))
            turn_far.append((stop, (k - 3) % COUNT))
        else:
            down.append((k, (k - 2) % COUNT))
            if core == 0:
                far.append((k, (k - 3) % COUNT))
    return up, down, far, turn_near, turn_far, swap


def unit_rows(values):
    norms = jnp.sqrt(jnp.sum(values * values, axis=-1, keepdims=True) + 1e-06)
    return (values / norms, norms)


def back_rows(unit, norms, grad_unit):
    along = jnp.sum(unit * grad_unit, axis=-1, keepdims=True)
    return (grad_unit - unit * along) / norms


def send(value, pairs):
    return lax.ppermute(value, AXES, pairs)


def local(images, texts, log_temp, bias):
    up, down, far, turn_near, turn_far, swap = routes()
    scale = jnp.exp(log_temp[0])
    shift_b = bias[0]
    count = images.shape[0]
    place_rows = lax.axis_index("rows")
    core = place_rows % CORES
    y = (place_rows // CORES) % Y
    first = core == 0
    img_unit, img_norm = unit_rows(images)
    txt_unit, txt_norm = unit_rows(texts)
    img = img_unit.astype(jnp.bfloat16)
    txt = txt_unit.astype(jnp.bfloat16)

    txt_up = send(txt, up)
    img_down = send(img, down)
    far_in = send(jnp.where(first, img, txt), far)
    beside = send(jnp.where(first, txt, img), swap)
    turned = send(jnp.where(first, img_down, txt_up), turn_near)
    turned_far = send(far_in, turn_far)
    txt_2 = jnp.where((y == 0) & (core == 1), turned, txt_up)
    img_2 = jnp.where((y == Y - 1) & (core == 0), turned, img_down)
    far_3 = jnp.where(((y == 1) & (core == 0)) | ((y == Y - 2) & (core == 1)), turned_far, far_in)
    txt_other = send(txt_2, swap)
    img_other = send(img_2, swap)
    txt_last = jnp.where(first, far_3, beside)
    img_last = jnp.where(first, beside, far_3)

    eye = jnp.eye(count, dtype=jnp.float32)

    def tile(left, right, sign):
        logits = scale * jnp.dot(left, right.T, preferred_element_type=jnp.float32) + shift_b
        loss = jnp.sum(jax.nn.softplus(-sign * logits), axis=-1)
        dlogit = (-sign * jax.nn.sigmoid(-sign * logits) * scale).astype(jnp.bfloat16)
        return loss, dlogit

    loss_sum, dlogit = tile(img, txt, 2.0 * eye - 1.0)
    img_grad = jnp.dot(dlogit, txt, preferred_element_type=jnp.float32)
    txt_grad = jnp.dot(dlogit.T, img, preferred_element_type=jnp.float32)
    for visit in (txt_last, txt_2, txt_other):
        loss, dlogit = tile(img, visit, -1.0)
        loss_sum = loss_sum + loss
        img_grad = img_grad + jnp.dot(dlogit, visit, preferred_element_type=jnp.float32)
    for visit in (img_last, img_2, img_other):
        _, dlogit = tile(visit, txt, -1.0)
        txt_grad = txt_grad + jnp.dot(dlogit.T, visit, preferred_element_type=jnp.float32)
    row_loss = loss_sum / (BAND * count)
    image_grad = back_rows(img_unit, img_norm, img_grad)
    text_grad = back_rows(txt_unit, txt_norm, txt_grad)
    return (row_loss, image_grad, text_grad)


def solution(mesh):
    placed = (P(AXES, None), P(AXES, None), P(), P())
    return jax.shard_map(
        local,
        mesh=mesh,
        in_specs=placed,
        out_specs=(P(AXES), P(AXES, None), P(AXES, None)),
        check_vma=False,
    )
```

```python
import functools

import jax
import jax.numpy as jnp
from jax import lax
from jax.experimental import pallas as pl
from jax.experimental.pallas import tpu as pltpu
from jax.sharding import PartitionSpec as P

BAND = 4
AXES = ("dp", "rows")
X, Y, Z, CORES = 4, 8, 12, 2
COUNT = X * Y * Z * CORES
Z_LO, Z_HI = 4, 3
HALF = jnp.bfloat16
WIDE = jnp.float32
PIECE = 64
LANES = 384


def place(k):
    core = k % CORES
    y = (k // CORES) % Y
    z_hi = (k // (CORES * Y)) % Z_HI
    x = (k // (CORES * Y * Z_HI)) % X
    z_lo = k // (CORES * Y * Z_HI * X)
    return x, y, z_hi * Z_LO + z_lo, core


INDEX = {place(k): k for k in range(COUNT)}


def routes():
    near, across, turned, far, far_turned, swap, pass_near, pass_turned = [], [], [], [], [], [], [], []
    for k in range(COUNT):
        x, y, z, core = place(k)
        edge = 7 if core == 1 else 0
        way = 1 if core == 1 else -1
        one, two, three = (k + way) % COUNT, (k + 2 * way) % COUNT, (k + 3 * way) % COUNT
        swap.append((k, k ^ 1))
        across.append((k, (k - 2 * way) % COUNT))
        if y == edge:
            stop = INDEX[(x, 7 - edge, z, core)]
            near.append((k, stop))
            turned.append((stop, two))
        else:
            near.append((k, two))
            if y != 7 - edge:
                far.append((k, one))
        if y == edge - way:
            turned.append((k, three))
        if y == 7 - edge:
            pass_turned.append((k, k ^ 1))
            far_turned.append((k, one))
        else:
            pass_near.append((k, k ^ 1))
    return near, across, turned, far, far_turned, swap, pass_near, pass_turned


def send(value, pairs):
    return lax.ppermute(value, AXES, pairs)


def rows_place():
    at = lax.axis_index("rows")
    return at % CORES, (at // CORES) % Y


def fetch(first, one, two, wide, sems, swap):
    count = wide.shape[0]

    def start(source):
        for i in range(count // PIECE):
            rows = pl.ds(i * PIECE, PIECE)
            pltpu.make_async_copy(source.at[rows], wide.at[rows], sems.at[i]).start()

    @pl.when(first != swap)
    def _():
        start(one)

    @pl.when(first == swap)
    def _():
        start(two)


def arrived(i, one, wide, sems):
    rows = pl.ds(i * PIECE, PIECE)
    pltpu.make_async_copy(one.at[rows], wide.at[rows], sems.at[i]).wait()
    return rows


def unit_kernel(swap, images, texts, half, norm, wide, sems):
    core, _ = rows_place()
    fetch(core == 0, images, texts, wide, sems, swap)
    for i in range(wide.shape[0] // PIECE):
        rows = arrived(i, images, wide, sems)
        values = wide[rows]
        size = jnp.sqrt(jnp.sum(values * values, axis=-1, keepdims=True) + 1e-06)
        norm[rows] = size
        half[rows] = (values / size).astype(HALF)


def tile(consts, own, other, diagonal, loss, logits, dlogit):
    scale, shift_b = jnp.exp(consts[0]), consts[1]
    logits[...] = lax.dot_general(own[...], other[...], (((1,), (1,)), ((), ())), preferred_element_type=WIDE)
    for i in range(logits.shape[0] // PIECE):
        rows = pl.ds(i * PIECE, PIECE)
        value = scale * logits[rows] + shift_b
        if diagonal:
            shape = value.shape
            same = lax.broadcasted_iota(jnp.int32, shape, 0) + i * PIECE == lax.broadcasted_iota(jnp.int32, shape, 1)
            value = jnp.where(same, -value, value)
        small = jnp.exp(-jnp.abs(value))
        loss[rows] += jnp.sum(jnp.maximum(value, 0.0) + jnp.log1p(small), axis=-1, keepdims=True)
        grad = jnp.where(value >= 0, 1.0, small) / (1.0 + small) * scale
        if diagonal:
            grad = jnp.where(same, -grad, grad)
        dlogit[rows] = grad.astype(HALF)


def add_grad(grad, dlogit, other, fresh=False):
    for i in range(grad.shape[1] // LANES):
        cols = pl.ds(i * LANES, LANES)
        part = jnp.dot(dlogit[...], other[:, cols], preferred_element_type=WIDE)
        grad[:, cols] = part if fresh else grad[:, cols] + part


def first_kernel(consts, u, v, beside, across, passed, grad_u, grad_v, loss_u, loss_v, logits, dlogit):
    loss_u[...] = jnp.zeros_like(loss_u)
    loss_v[...] = jnp.zeros_like(loss_v)
    for own, grad, loss, others in ((u, grad_u, loss_u, (v, across)), (v, grad_v, loss_v, (u, beside, passed))):
        for i, other in enumerate(others):
            tile(consts, own, other, i == 0, loss, logits, dlogit)
            add_grad(grad, dlogit, other, i == 0)


def back(rows, values, norm, grad):
    size = norm[rows]
    unit = values / size
    value = grad[rows]
    along = jnp.sum(unit * value, axis=-1, keepdims=True)
    return (value - unit * along) / size


def second_kernel(consts, v, near, turned, images, texts, norm_v, grad_v_in, loss_v_in, grad_v, loss_v,
                  logits, dlogit, block, wide, sems):
    core, y = rows_place()
    fetch(core == 0, images, texts, wide, sems, True)
    edge = jnp.where(core == 0, 7, 0)
    loss_v[...] = loss_v_in[...]
    grad_v[...] = grad_v_in[...]
    block[...] = jnp.where(y == edge, turned[...], near[...])
    tile(consts, v, block, False, loss_v, logits, dlogit)
    add_grad(grad_v, dlogit, block)
    for i in range(wide.shape[0] // PIECE):
        rows = arrived(i, images, wide, sems)
        grad_v[rows] = back(rows, wide[rows], norm_v, grad_v)


def last_kernel(consts, u, passed, passed_turned, far, leap, far_turned, images, texts, norm_u, grad_u_in, grad_v, loss_u_in,
                loss_v, row_loss, image_grad, text_grad, grad_u, loss_u, logits, dlogit, block, wide, sems, out_sems, v_sem):
    core, y = rows_place()
    count = wide.shape[0]
    pieces = count // PIECE
    fetch(core == 0, images, texts, wide, sems, False)

    @pl.when(core == 0)
    def _():
        pltpu.make_async_copy(grad_v, text_grad, v_sem).start()

    @pl.when(core != 0)
    def _():
        pltpu.make_async_copy(grad_v, image_grad, v_sem).start()

    edge, after = jnp.where(core == 0, 0, 7), jnp.where(core == 0, 1, 6)
    loss_u[...] = loss_u_in[...]
    grad_u[...] = grad_u_in[...]
    block[...] = jnp.where(y == edge, passed_turned[...], passed[...])
    tile(consts, u, block, False, loss_u, logits, dlogit)
    add_grad(grad_u, dlogit, block)
    block[...] = jnp.where(y == edge, leap[...], jnp.where(y == after, far_turned[...], far[...]))
    tile(consts, u, block, False, loss_u, logits, dlogit)
    add_grad(grad_u, dlogit, block)
    for i in range(pieces):
        rows = arrived(i, images, wide, sems)
        grad_u[rows] = back(rows, wide[rows], norm_u, grad_u)

        @pl.when(core == 0)
        def _():
            pltpu.make_async_copy(grad_u.at[rows], image_grad.at[rows], out_sems.at[i]).start()

        @pl.when(core != 0)
        def _():
            pltpu.make_async_copy(grad_u.at[rows], text_grad.at[rows], out_sems.at[i]).start()

    total = jnp.where(core == 0, loss_u[...], loss_v[...]) / (BAND * count)
    row_loss[...] = jnp.broadcast_to(total, (count, 128)).T[0:1]
    for i in range(pieces):
        rows = pl.ds(i * PIECE, PIECE)
        pltpu.make_async_copy(grad_u.at[rows], image_grad.at[rows], out_sems.at[i]).wait()
    pltpu.make_async_copy(grad_v, text_grad, v_sem).wait()


VMEM = pl.BlockSpec(memory_space=pltpu.VMEM)
SMEM = pl.BlockSpec(memory_space=pltpu.SMEM)
HBM = pl.BlockSpec(memory_space=pltpu.HBM)
PARAMS = pltpu.CompilerParams(vmem_limit_bytes=24 * 2**20)


def cost(tiles):
    return pl.CostEstimate(flops=tiles * 40 * 256 * 256 * 1152, bytes_accessed=4 * 2**20, transcendentals=0)


def local(images, texts, log_temp, bias):
    near_to, across_to, turned_to, far_to, far_turned_to, swap_to, pass_near_to, pass_turned_to = routes()
    count, width = images.shape
    pieces = count // PIECE
    consts = jnp.concatenate([log_temp, bias])
    half = jax.ShapeDtypeStruct((count, width), HALF)
    wide = jax.ShapeDtypeStruct((count, width), WIDE)
    column = jax.ShapeDtypeStruct((count, 1), WIDE)
    logits = pltpu.VMEM((count, count), WIDE)
    dlogit = pltpu.VMEM((count, count), HALF)
    half_room = pltpu.VMEM((count, width), HALF)
    wide_room = pltpu.VMEM((count, width), WIDE)
    column_room = pltpu.VMEM((count, 1), WIDE)
    sems = pltpu.SemaphoreType.DMA((pieces,))

    def unit(swap):
        return pl.pallas_call(
            functools.partial(unit_kernel, swap),
            out_shape=(half, column),
            in_specs=[HBM, HBM],
            out_specs=(VMEM, VMEM),
            scratch_shapes=[wide_room, sems],
            compiler_params=PARAMS,
        )(images, texts)

    _, y = rows_place()
    u, norm_u = unit(False)
    near = send(u, near_to)
    v, norm_v = unit(True)
    across = send(v, across_to)
    turned = send(jnp.where((y == 0) | (y == 7), near, u), turned_to)
    beside = send(v, swap_to)
    far = send(near, far_to)
    passed_near = send(near, pass_near_to)
    passed_across = send(across, swap_to)
    far_turned = send(turned, far_turned_to)
    passed_turned = send(turned, pass_turned_to)

    grad_u, grad_v, loss_u, loss_v = pl.pallas_call(
        first_kernel,
        out_shape=(wide, wide, column, column),
        in_specs=[SMEM] + [VMEM] * 5,
        out_specs=(VMEM,) * 4,
        scratch_shapes=[logits, dlogit],
        compiler_params=PARAMS,
        cost_estimate=cost(5),
    )(consts, u, v, beside, across, passed_across)
    grad_v, loss_v = pl.pallas_call(
        second_kernel,
        out_shape=(wide, column),
        in_specs=[SMEM] + [VMEM] * 3 + [HBM] * 2 + [VMEM] * 3,
        out_specs=(VMEM,) * 2,
        scratch_shapes=[logits, dlogit, half_room, wide_room, sems],
        compiler_params=PARAMS,
        cost_estimate=cost(1),
    )(consts, v, near, turned, images, texts, norm_v, grad_v, loss_v)
    row_loss, image_grad, text_grad = pl.pallas_call(
        last_kernel,
        out_shape=(jax.ShapeDtypeStruct((1, count), WIDE), wide, wide),
        in_specs=[SMEM] + [VMEM] * 6 + [HBM] * 2 + [VMEM] * 5,
        out_specs=(VMEM, HBM, HBM),
        scratch_shapes=[wide_room, column_room, logits, dlogit, half_room, wide_room, sems, sems, pltpu.SemaphoreType.DMA],
        compiler_params=PARAMS,
        cost_estimate=cost(2),
    )(consts, u, passed_near, passed_turned, far, turned, far_turned, images, texts, norm_u, grad_u, grad_v, loss_u, loss_v)
    return (row_loss.reshape(count), image_grad, text_grad)


def solution(mesh):
    placed = (P(AXES, None), P(AXES, None), P(), P())
    return jax.shard_map(
        local,
        mesh=mesh,
        in_specs=placed,
        out_specs=(P(AXES), P(AXES, None), P(AXES, None)),
        check_vma=False,
    )
```

```python
import functools

import jax
import jax.numpy as jnp
from jax import lax
from jax.experimental import pallas as pl
from jax.experimental.pallas import tpu as pltpu
from jax.sharding import PartitionSpec as P

BAND = 4
AXES = ("dp", "rows")
X, Y, Z, CORES = 4, 8, 12, 2
COUNT = X * Y * Z * CORES
Z_LO, Z_HI = 4, 3
HALF = jnp.bfloat16
WIDE = jnp.float32
PIECE = 64
LANES = 384


def place(k):
    core = k % CORES
    y = (k // CORES) % Y
    z_hi = (k // (CORES * Y)) % Z_HI
    x = (k // (CORES * Y * Z_HI)) % X
    z_lo = k // (CORES * Y * Z_HI * X)
    return x, y, z_hi * Z_LO + z_lo, core


INDEX = {place(k): k for k in range(COUNT)}


def routes():
    names = ("near", "across", "turned", "far", "far_turned", "swap", "pass_near", "pass_turned")
    pairs = {name: [] for name in names}
    for k in range(COUNT):
        x, y, z, core = place(k)
        edge = 7 if core == 1 else 0
        way = 1 if core == 1 else -1
        one, two, three = (k + way) % COUNT, (k + 2 * way) % COUNT, (k + 3 * way) % COUNT
        pairs["swap"].append((k, k ^ 1))
        pairs["across"].append((k, (k - 2 * way) % COUNT))
        if y == edge:
            stop = INDEX[(place(two)[0], 7 - edge, z, core)]
            pairs["near"].append((k, stop))
            pairs["turned"].append((stop, two))
        else:
            pairs["near"].append((k, two))
            if y != 7 - edge:
                pairs["far"].append((k, one))
        if y == edge - way:
            pairs["turned"].append((k, three))
        if y == 7 - edge:
            pairs["pass_turned"].append((k, k ^ 1))
            pairs["far_turned"].append((k, one))
        else:
            pairs["pass_near"].append((k, k ^ 1))
    return pairs


def send(value, pairs):
    return lax.ppermute(value, AXES, pairs)


def rows_place():
    at = lax.axis_index("rows")
    return at % CORES, (at // CORES) % Y


def fetch(first, one, two, wide, sems, swap):
    count = wide.shape[0]

    def start(source):
        for i in range(count // PIECE):
            rows = pl.ds(i * PIECE, PIECE)
            pltpu.make_async_copy(source.at[rows], wide.at[rows], sems.at[i]).start()

    @pl.when(first != swap)
    def _():
        start(one)

    @pl.when(first == swap)
    def _():
        start(two)


def arrived(i, one, wide, sems):
    rows = pl.ds(i * PIECE, PIECE)
    pltpu.make_async_copy(one.at[rows], wide.at[rows], sems.at[i]).wait()
    return rows


def unit_kernel(swap, images, texts, half, norm, wide, sems):
    core, _ = rows_place()
    fetch(core == 0, images, texts, wide, sems, swap)
    for i in range(wide.shape[0] // PIECE):
        rows = arrived(i, images, wide, sems)
        values = wide[rows]
        size = jnp.sqrt(jnp.sum(values * values, axis=-1, keepdims=True) + 1e-06)
        norm[rows] = size
        half[rows] = (values * (1.0 / size)).astype(HALF)


def gate_kernel(*refs):
    pass


def after(value, *others):
    return pl.pallas_call(
        gate_kernel,
        out_shape=jax.ShapeDtypeStruct(value.shape, value.dtype),
        in_specs=[HBM] * (1 + len(others)),
        out_specs=HBM,
        input_output_aliases={0: 0},
        compiler_params=PARAMS,
    )(value, *others)


def tile(consts, own, other, diagonal, loss, logits, dlogit):
    scale, shift_b = jnp.exp(consts[0]), consts[1]
    logits[...] = lax.dot_general(own[...], other[...], (((1,), (1,)), ((), ())), preferred_element_type=WIDE)
    for i in range(logits.shape[0] // PIECE):
        rows = pl.ds(i * PIECE, PIECE)
        value = scale * logits[rows] + shift_b
        if diagonal:
            shape = value.shape
            same = lax.broadcasted_iota(jnp.int32, shape, 0) + i * PIECE == lax.broadcasted_iota(jnp.int32, shape, 1)
            value = jnp.where(same, -value, value)
        small = jnp.exp(-jnp.abs(value))
        loss[rows] += jnp.sum(jnp.maximum(value, 0.0) + jnp.log(1.0 + small), axis=-1, keepdims=True)
        grad = jnp.where(value >= 0, scale, scale * small) * pl.reciprocal(1.0 + small)
        if diagonal:
            grad = jnp.where(same, -grad, grad)
        dlogit[rows] = grad.astype(HALF)


def add_grad(grad, dlogit, other, fresh=False, base=None):
    for i in range(grad.shape[1] // LANES):
        cols = pl.ds(i * LANES, LANES)
        part = jnp.dot(dlogit[...], other[:, cols], preferred_element_type=WIDE)
        grad[:, cols] = part if fresh else (grad if base is None else base)[:, cols] + part


def first_kernel(consts, u, v, grad_u, grad_v, loss_u, loss_v, logits, dlogit):
    loss_u[...] = jnp.zeros_like(loss_u)
    loss_v[...] = jnp.zeros_like(loss_v)
    for own, grad, loss, others in ((u, grad_u, loss_u, (v,)), (v, grad_v, loss_v, (u,))):
        for i, other in enumerate(others):
            tile(consts, own, other, i == 0, loss, logits, dlogit)
            add_grad(grad, dlogit, other, i == 0)


def back(rows, values, norm, grad):
    inverse = 1.0 / norm[rows]
    value = grad[rows]
    along = jnp.sum(values * value, axis=-1, keepdims=True) * (inverse * inverse)
    return (value - values * along) * inverse


def second_kernel(consts, u, v, beside, across, passed, near, turned, images, texts, norm_v, grad_u_in, grad_v_in, loss_u_in,
                  loss_v_in, grad_u, grad_v, loss_u, loss_v, logits, dlogit, block, wide, sems):
    core, y = rows_place()
    fetch(core == 0, images, texts, wide, sems, True)
    loss_u[...] = loss_u_in[...]
    loss_v[...] = loss_v_in[...]
    tile(consts, u, across, False, loss_u, logits, dlogit)
    add_grad(grad_u, dlogit, across, base=grad_u_in)
    tile(consts, v, beside, False, loss_v, logits, dlogit)
    add_grad(grad_v, dlogit, beside, base=grad_v_in)
    tile(consts, v, passed, False, loss_v, logits, dlogit)
    add_grad(grad_v, dlogit, passed)
    block[...] = jnp.where(y == jnp.where(core == 0, 7, 0), turned[...], near[...])
    tile(consts, v, block, False, loss_v, logits, dlogit)
    add_grad(grad_v, dlogit, block)
    for i in range(wide.shape[0] // PIECE):
        rows = arrived(i, images, wide, sems)
        grad_v[rows] = back(rows, wide[rows], norm_v, grad_v)


def last_kernel(consts, u, passed, passed_turned, far, leap, far_turned, images, texts, norm_u, grad_u_in, grad_v, loss_u_in,
                loss_v, row_loss, image_grad, text_grad, grad_u, loss_u, logits, dlogit, block, wide, sems, out_sems, v_sem):
    core, y = rows_place()
    count = wide.shape[0]
    pieces = count // PIECE
    fetch(core == 0, images, texts, wide, sems, False)

    @pl.when(core == 0)
    def _():
        pltpu.make_async_copy(grad_v, text_grad, v_sem).start()

    @pl.when(core != 0)
    def _():
        pltpu.make_async_copy(grad_v, image_grad, v_sem).start()

    edge, after = jnp.where(core == 0, 0, 7), jnp.where(core == 0, 1, 6)
    loss_u[...] = loss_u_in[...]
    block[...] = jnp.where(y == edge, passed_turned[...], passed[...])
    tile(consts, u, block, False, loss_u, logits, dlogit)
    add_grad(grad_u, dlogit, block, base=grad_u_in)
    block[...] = jnp.where(y == edge, leap[...], jnp.where(y == after, far_turned[...], far[...]))
    tile(consts, u, block, False, loss_u, logits, dlogit)
    add_grad(grad_u, dlogit, block)
    for i in range(pieces):
        rows = arrived(i, images, wide, sems)
        grad_u[rows] = back(rows, wide[rows], norm_u, grad_u)

        @pl.when(core == 0)
        def _():
            pltpu.make_async_copy(grad_u.at[rows], image_grad.at[rows], out_sems.at[i]).start()

        @pl.when(core != 0)
        def _():
            pltpu.make_async_copy(grad_u.at[rows], text_grad.at[rows], out_sems.at[i]).start()

    total = jnp.where(core == 0, loss_u[...], loss_v[...]) / (BAND * count)
    row_loss[...] = jnp.broadcast_to(total, (count, 128)).T[0:1]
    for i in range(pieces):
        rows = pl.ds(i * PIECE, PIECE)
        pltpu.make_async_copy(grad_u.at[rows], image_grad.at[rows], out_sems.at[i]).wait()
    pltpu.make_async_copy(grad_v, text_grad, v_sem).wait()


VMEM = pl.BlockSpec(memory_space=pltpu.VMEM)
SMEM = pl.BlockSpec(memory_space=pltpu.SMEM)
HBM = pl.BlockSpec(memory_space=pl.ANY)
PARAMS = pltpu.CompilerParams(vmem_limit_bytes=24 * 2**20)


def cost(tiles):
    return pl.CostEstimate(flops=int(tiles * 40) * 256 * 256 * 1152, bytes_accessed=4 * 2**20, transcendentals=0)


def local(images, texts, log_temp, bias):
    pairs = routes()
    count, width = images.shape
    pieces = count // PIECE
    consts = jnp.concatenate([log_temp, bias])
    half = jax.ShapeDtypeStruct((count, width), HALF)
    wide = jax.ShapeDtypeStruct((count, width), WIDE)
    column = jax.ShapeDtypeStruct((count, 1), WIDE)
    logits = pltpu.VMEM((count, count), WIDE)
    dlogit = pltpu.VMEM((count, count), HALF)
    half_room = pltpu.VMEM((count, width), HALF)
    wide_room = pltpu.VMEM((count, width), WIDE)
    column_room = pltpu.VMEM((count, 1), WIDE)
    sems = pltpu.SemaphoreType.DMA((pieces,))

    def unit(swap, room):
        return pl.pallas_call(
            functools.partial(unit_kernel, swap),
            out_shape=(half, column),
            in_specs=[HBM, HBM],
            out_specs=(VMEM, VMEM),
            scratch_shapes=[wide_room, sems],
            compiler_params=pltpu.CompilerParams(vmem_limit_bytes=room * 2**20),
        )(images, texts)

    _, y = rows_place()
    u, norm_u = unit(False, 24)
    near = send(u, pairs["near"])
    v, norm_v = unit(True, 24)
    across = send(v, pairs["across"])
    turned = send(jnp.where((y == 0) | (y == 7), near, u), pairs["turned"])
    beside = send(v, pairs["swap"])
    far = send(near, pairs["far"])
    passed_near = send(near, pairs["pass_near"])
    passed_across = send(across, pairs["swap"])
    grad_u, grad_v, loss_u, loss_v = pl.pallas_call(
        first_kernel,
        out_shape=(wide, wide, column, column),
        in_specs=[SMEM] + [VMEM] * 2,
        out_specs=(VMEM,) * 4,
        scratch_shapes=[logits, dlogit],
        compiler_params=PARAMS,
        cost_estimate=cost(0.1),
    )(consts, u, v)
    turned = after(turned, loss_u, far, passed_near)
    far_turned = send(turned, pairs["far_turned"])
    passed_turned = send(turned, pairs["pass_turned"])
    grad_u, grad_v, loss_u, loss_v = pl.pallas_call(
        second_kernel,
        out_shape=(wide, wide, column, column),
        in_specs=[SMEM] + [VMEM] * 7 + [HBM] * 2 + [VMEM] * 5,
        out_specs=(VMEM,) * 4,
        scratch_shapes=[logits, dlogit, half_room, wide_room, sems],
        compiler_params=PARAMS,
        cost_estimate=cost(3),
    )(consts, u, v, beside, across, passed_across, near, turned, images, texts, norm_v, grad_u, grad_v, loss_u, loss_v)
    row_loss, image_grad, text_grad = pl.pallas_call(
        last_kernel,
        out_shape=(jax.ShapeDtypeStruct((1, count), WIDE), wide, wide),
        in_specs=[SMEM] + [VMEM] * 6 + [HBM] * 2 + [VMEM] * 5,
        out_specs=(VMEM, HBM, HBM),
        scratch_shapes=[wide_room, column_room, logits, dlogit, half_room, wide_room, sems, sems, pltpu.SemaphoreType.DMA],
        compiler_params=PARAMS,
        cost_estimate=cost(2),
    )(consts, u, passed_near, passed_turned, far, turned, far_turned, images, texts, norm_u, grad_u, grad_v, loss_u, loss_v)
    return (row_loss.reshape(count), image_grad, text_grad)


def solution(mesh):
    placed = (P(AXES, None), P(AXES, None), P(), P())
    return jax.shard_map(
        local,
        mesh=mesh,
        in_specs=placed,
        out_specs=(P(AXES), P(AXES, None), P(AXES, None)),
        check_vma=False,
    )
```

```python
import functools

import jax
import jax.numpy as jnp
from jax import lax
from jax.experimental import pallas as pl
from jax.experimental.pallas import tpu as pltpu
from jax.sharding import PartitionSpec as P

BAND = 4
AXES = ("dp", "rows")
X, Y, Z, CORES = 4, 8, 12, 2
COUNT = X * Y * Z * CORES
Z_LO, Z_HI = 4, 3
HALF = jnp.bfloat16
WIDE = jnp.float32
PIECE = 64
LANES = 384


def place(k):
    core = k % CORES
    y = (k // CORES) % Y
    z_hi = (k // (CORES * Y)) % Z_HI
    x = (k // (CORES * Y * Z_HI)) % X
    z_lo = k // (CORES * Y * Z_HI * X)
    return x, y, z_hi * Z_LO + z_lo, core


INDEX = {place(k): k for k in range(COUNT)}


def routes():
    names = ("near", "across", "leap", "turned", "far", "far_turned", "swap", "pass_near", "pass_turned")
    pairs = {name: [] for name in names}
    for k in range(COUNT):
        x, y, z, core = place(k)
        edge = 7 if core == 1 else 0
        way = 1 if core == 1 else -1
        one, two, three = (k + way) % COUNT, (k + 2 * way) % COUNT, (k + 3 * way) % COUNT
        pairs["swap"].append((k, k ^ 1))
        pairs["across"].append((k, (k - 2 * way) % COUNT))
        if y == edge:
            stop = INDEX[(place(two)[0], 7 - edge, z, core)]
            pairs["near"].append((k, stop))
            pairs["turned"].append((stop, two))
        else:
            pairs["near"].append((k, two))
            if y != 7 - edge:
                pairs["far"].append((k, one))
        if y == edge - way:
            pairs["leap"].append((k, three))
        if y == 7 - edge:
            pairs["pass_turned"].append((k, k ^ 1))
            pairs["far_turned"].append((k, one))
        else:
            pairs["pass_near"].append((k, k ^ 1))
    return pairs


def send(value, pairs):
    return lax.ppermute(value, AXES, pairs)


def rows_place():
    at = lax.axis_index("rows")
    return at % CORES, (at // CORES) % Y


def fetch(first, one, two, wide, sems, swap):
    count = wide.shape[0]

    def start(source):
        for i in range(count // PIECE):
            rows = pl.ds(i * PIECE, PIECE)
            pltpu.make_async_copy(source.at[rows], wide.at[rows], sems.at[i]).start()

    @pl.when(first != swap)
    def _():
        start(one)

    @pl.when(first == swap)
    def _():
        start(two)


def arrived(i, one, wide, sems):
    rows = pl.ds(i * PIECE, PIECE)
    pltpu.make_async_copy(one.at[rows], wide.at[rows], sems.at[i]).wait()
    return rows


def unit_kernel(swap, images, texts, half, norm, wide, sems):
    core, _ = rows_place()
    fetch(core == 0, images, texts, wide, sems, swap)
    for i in range(wide.shape[0] // PIECE):
        rows = arrived(i, images, wide, sems)
        values = wide[rows]
        size = jnp.sqrt(jnp.sum(values * values, axis=-1, keepdims=True) + 1e-06)
        norm[rows] = size
        half[rows] = (values * (1.0 / size)).astype(HALF)


def gate_kernel(*refs):
    pass


def after(value, *others, flops=0):
    return pl.pallas_call(
        gate_kernel,
        out_shape=jax.ShapeDtypeStruct(value.shape, value.dtype),
        in_specs=[HBM] * (1 + len(others)),
        out_specs=HBM,
        input_output_aliases={0: 0},
        compiler_params=PARAMS,
        cost_estimate=pl.CostEstimate(flops=flops, bytes_accessed=0, transcendentals=0),
    )(value, *others)


def tile(consts, own, other, diagonal, loss, logits, dlogit):
    scale, shift_b = jnp.exp(consts[0]), consts[1]
    logits[...] = lax.dot_general(own[...], other[...], (((1,), (1,)), ((), ())), preferred_element_type=WIDE)
    for i in range(logits.shape[0] // PIECE):
        rows = pl.ds(i * PIECE, PIECE)
        value = scale * logits[rows] + shift_b
        if diagonal:
            shape = value.shape
            same = lax.broadcasted_iota(jnp.int32, shape, 0) + i * PIECE == lax.broadcasted_iota(jnp.int32, shape, 1)
            value = jnp.where(same, -value, value)
        small = jnp.exp(-jnp.abs(value))
        loss[rows] += jnp.sum(jnp.maximum(value, 0.0) + jnp.log(1.0 + small), axis=-1, keepdims=True)
        grad = jnp.where(value >= 0, scale, scale * small) * pl.reciprocal(1.0 + small)
        if diagonal:
            grad = jnp.where(same, -grad, grad)
        dlogit[rows] = grad.astype(HALF)


def add_grad(grad, dlogit, other, fresh=False, base=None):
    for i in range(grad.shape[1] // LANES):
        cols = pl.ds(i * LANES, LANES)
        part = jnp.dot(dlogit[...], other[:, cols], preferred_element_type=WIDE)
        grad[:, cols] = part if fresh else (grad if base is None else base)[:, cols] + part


def first_kernel(consts, u, v, grad_u, grad_v, loss_u, loss_v, logits, dlogit):
    loss_u[...] = jnp.zeros_like(loss_u)
    loss_v[...] = jnp.zeros_like(loss_v)
    for own, grad, loss, others in ((u, grad_u, loss_u, (v,)), (v, grad_v, loss_v, (u,))):
        for i, other in enumerate(others):
            tile(consts, own, other, i == 0, loss, logits, dlogit)
            add_grad(grad, dlogit, other, i == 0)


def back(rows, values, norm, grad):
    inverse = 1.0 / norm[rows]
    value = grad[rows]
    along = jnp.sum(values * value, axis=-1, keepdims=True) * (inverse * inverse)
    return (value - values * along) * inverse


def second_kernel(consts, u, v, beside, across, passed, near, turned, images, texts, norm_v, grad_u_in, grad_v_in, loss_u_in,
                  loss_v_in, grad_u, grad_v, loss_u, loss_v, logits, dlogit, block, wide, sems):
    core, y = rows_place()
    fetch(core == 0, images, texts, wide, sems, True)
    loss_u[...] = loss_u_in[...]
    loss_v[...] = loss_v_in[...]
    tile(consts, u, across, False, loss_u, logits, dlogit)
    add_grad(grad_u, dlogit, across, base=grad_u_in)
    tile(consts, v, beside, False, loss_v, logits, dlogit)
    add_grad(grad_v, dlogit, beside, base=grad_v_in)
    tile(consts, v, passed, False, loss_v, logits, dlogit)
    add_grad(grad_v, dlogit, passed)
    block[...] = jnp.where(y == jnp.where(core == 0, 7, 0), turned[...], near[...])
    tile(consts, v, block, False, loss_v, logits, dlogit)
    add_grad(grad_v, dlogit, block)
    for i in range(wide.shape[0] // PIECE):
        rows = arrived(i, images, wide, sems)
        grad_v[rows] = back(rows, wide[rows], norm_v, grad_v)


def last_kernel(consts, u, passed, passed_turned, far, leap, far_turned, images, texts, norm_u, grad_u_in, grad_v, loss_u_in,
                loss_v, row_loss, image_grad, text_grad, grad_u, loss_u, logits, dlogit, block, wide, sems, out_sems, v_sem):
    core, y = rows_place()
    count = wide.shape[0]
    pieces = count // PIECE
    fetch(core == 0, images, texts, wide, sems, False)

    @pl.when(core == 0)
    def _():
        pltpu.make_async_copy(grad_v, text_grad, v_sem).start()

    @pl.when(core != 0)
    def _():
        pltpu.make_async_copy(grad_v, image_grad, v_sem).start()

    edge, after = jnp.where(core == 0, 0, 7), jnp.where(core == 0, 1, 6)
    loss_u[...] = loss_u_in[...]
    block[...] = jnp.where(y == edge, passed_turned[...], passed[...])
    tile(consts, u, block, False, loss_u, logits, dlogit)
    add_grad(grad_u, dlogit, block, base=grad_u_in)
    block[...] = jnp.where(y == edge, leap[...], jnp.where(y == after, far_turned[...], far[...]))
    tile(consts, u, block, False, loss_u, logits, dlogit)
    add_grad(grad_u, dlogit, block)
    for i in range(pieces):
        rows = arrived(i, images, wide, sems)
        grad_u[rows] = back(rows, wide[rows], norm_u, grad_u)

        @pl.when(core == 0)
        def _():
            pltpu.make_async_copy(grad_u.at[rows], image_grad.at[rows], out_sems.at[i]).start()

        @pl.when(core != 0)
        def _():
            pltpu.make_async_copy(grad_u.at[rows], text_grad.at[rows], out_sems.at[i]).start()

    total = jnp.where(core == 0, loss_u[...], loss_v[...]) / (BAND * count)
    row_loss[...] = jnp.broadcast_to(total, (count, 128)).T[0:1]
    for i in range(pieces):
        rows = pl.ds(i * PIECE, PIECE)
        pltpu.make_async_copy(grad_u.at[rows], image_grad.at[rows], out_sems.at[i]).wait()
    pltpu.make_async_copy(grad_v, text_grad, v_sem).wait()


VMEM = pl.BlockSpec(memory_space=pltpu.VMEM)
SMEM = pl.BlockSpec(memory_space=pltpu.SMEM)
HBM = pl.BlockSpec(memory_space=pl.ANY)
PARAMS = pltpu.CompilerParams(vmem_limit_bytes=24 * 2**20)


def cost(tiles):
    return pl.CostEstimate(flops=int(tiles * 40) * 256 * 256 * 1152, bytes_accessed=4 * 2**20, transcendentals=0)


def local(images, texts, log_temp, bias):
    pairs = routes()
    count, width = images.shape
    pieces = count // PIECE
    consts = jnp.concatenate([log_temp, bias])
    half = jax.ShapeDtypeStruct((count, width), HALF)
    wide = jax.ShapeDtypeStruct((count, width), WIDE)
    column = jax.ShapeDtypeStruct((count, 1), WIDE)
    logits = pltpu.VMEM((count, count), WIDE)
    dlogit = pltpu.VMEM((count, count), HALF)
    half_room = pltpu.VMEM((count, width), HALF)
    wide_room = pltpu.VMEM((count, width), WIDE)
    column_room = pltpu.VMEM((count, 1), WIDE)
    sems = pltpu.SemaphoreType.DMA((pieces,))

    def unit(swap, room):
        return pl.pallas_call(
            functools.partial(unit_kernel, swap),
            out_shape=(half, column),
            in_specs=[HBM, HBM],
            out_specs=(VMEM, VMEM),
            scratch_shapes=[wide_room, sems],
            compiler_params=pltpu.CompilerParams(vmem_limit_bytes=room * 2**20),
        )(images, texts)

    u, norm_u = unit(False, 24)
    near = send(u, pairs["near"])
    v, norm_v = unit(True, 24)
    across = send(v, pairs["across"])
    turned = send(near, pairs["turned"])
    leap = send(u, pairs["leap"])
    beside = send(after(v, near), pairs["swap"])
    far = send(near, pairs["far"])
    passed_near = send(near, pairs["pass_near"])
    grad_u, grad_v, loss_u, loss_v = pl.pallas_call(
        first_kernel,
        out_shape=(wide, wide, column, column),
        in_specs=[SMEM] + [VMEM] * 2,
        out_specs=(VMEM,) * 4,
        scratch_shapes=[logits, dlogit],
        compiler_params=PARAMS,
        cost_estimate=cost(0.1),
    )(consts, u, v)
    across = after(across, leap, loss_u)
    passed_across = send(across, pairs["swap"])
    turned = after(turned, flops=35 * 10**8)
    turned = after(turned, far, passed_near, beside)
    far_turned = send(turned, pairs["far_turned"])
    passed_turned = send(turned, pairs["pass_turned"])
    grad_u, grad_v, loss_u, loss_v = pl.pallas_call(
        second_kernel,
        out_shape=(wide, wide, column, column),
        in_specs=[SMEM] + [VMEM] * 7 + [HBM] * 2 + [VMEM] * 5,
        out_specs=(VMEM,) * 4,
        scratch_shapes=[logits, dlogit, half_room, wide_room, sems],
        compiler_params=PARAMS,
        cost_estimate=cost(3),
    )(consts, u, v, beside, across, passed_across, near, turned, images, texts, norm_v, grad_u, grad_v, loss_u, loss_v)
    row_loss, image_grad, text_grad = pl.pallas_call(
        last_kernel,
        out_shape=(jax.ShapeDtypeStruct((1, count), WIDE), wide, wide),
        in_specs=[SMEM] + [VMEM] * 6 + [HBM] * 2 + [VMEM] * 5,
        out_specs=(VMEM, HBM, HBM),
        scratch_shapes=[wide_room, column_room, logits, dlogit, half_room, wide_room, sems, sems, pltpu.SemaphoreType.DMA],
        compiler_params=PARAMS,
        cost_estimate=cost(2),
    )(consts, u, passed_near, passed_turned, far, leap, far_turned, images, texts, norm_u, grad_u, grad_v, loss_u, loss_v)
    return (row_loss.reshape(count), image_grad, text_grad)


def solution(mesh):
    placed = (P(AXES, None), P(AXES, None), P(), P())
    return jax.shard_map(
        local,
        mesh=mesh,
        in_specs=placed,
        out_specs=(P(AXES), P(AXES, None), P(AXES, None)),
        check_vma=False,
    )
```

```python
import functools

import jax
import jax.numpy as jnp
from jax import lax
from jax.experimental import pallas as pl
from jax.experimental.pallas import tpu as pltpu
from jax.sharding import PartitionSpec as P

BAND = 4
AXES = ("dp", "rows")
X, Y, Z, CORES = 4, 8, 12, 2
COUNT = X * Y * Z * CORES
Z_LO, Z_HI = 4, 3
HALF = jnp.bfloat16
WIDE = jnp.float32
PIECE = 64
LANES = 384


def place(k):
    core = k % CORES
    y = (k // CORES) % Y
    z_hi = (k // (CORES * Y)) % Z_HI
    x = (k // (CORES * Y * Z_HI)) % X
    z_lo = k // (CORES * Y * Z_HI * X)
    return x, y, z_hi * Z_LO + z_lo, core


INDEX = {place(k): k for k in range(COUNT)}


def routes():
    names = ("near", "across", "leap", "turned", "far", "far_turned", "swap", "pass_near", "pass_turned")
    pairs = {name: [] for name in names}
    for k in range(COUNT):
        x, y, z, core = place(k)
        edge = 7 if core == 1 else 0
        way = 1 if core == 1 else -1
        one, two, three = (k + way) % COUNT, (k + 2 * way) % COUNT, (k + 3 * way) % COUNT
        pairs["swap"].append((k, k ^ 1))
        pairs["across"].append((k, (k - 2 * way) % COUNT))
        if y == edge:
            stop = INDEX[(place(two)[0], 7 - edge, z, core)]
            pairs["near"].append((k, stop))
            pairs["turned"].append((stop, two))
        else:
            pairs["near"].append((k, two))
            if y != 7 - edge:
                pairs["far"].append((k, one))
        if y == edge - way:
            pairs["leap"].append((k, three))
        if y == 7 - edge:
            pairs["pass_turned"].append((k, k ^ 1))
            pairs["far_turned"].append((k, one))
        else:
            pairs["pass_near"].append((k, k ^ 1))
    return pairs


def send(value, pairs):
    return lax.ppermute(value, AXES, pairs)


def rows_place():
    at = lax.axis_index("rows")
    return at % CORES, (at // CORES) % Y


def fetch(first, one, two, wide, sems, swap):
    count = wide.shape[0]

    def start(source):
        for i in range(count // PIECE):
            rows = pl.ds(i * PIECE, PIECE)
            pltpu.make_async_copy(source.at[rows], wide.at[rows], sems.at[i]).start()

    @pl.when(first != swap)
    def _():
        start(one)

    @pl.when(first == swap)
    def _():
        start(two)


def arrived(i, one, wide, sems):
    rows = pl.ds(i * PIECE, PIECE)
    pltpu.make_async_copy(one.at[rows], wide.at[rows], sems.at[i]).wait()
    return rows


def unit_kernel(swap, images, texts, half, norm, wide, sems):
    core, _ = rows_place()
    fetch(core == 0, images, texts, wide, sems, swap)
    for i in range(wide.shape[0] // PIECE):
        rows = arrived(i, images, wide, sems)
        values = wide[rows]
        size = jnp.sqrt(jnp.sum(values * values, axis=-1, keepdims=True) + 1e-06)
        norm[rows] = size
        half[rows] = (values * (1.0 / size)).astype(HALF)


def gate_kernel(*refs):
    pass


def after(value, *others, flops=0):
    return pl.pallas_call(
        gate_kernel,
        out_shape=jax.ShapeDtypeStruct(value.shape, value.dtype),
        in_specs=[HBM] * (1 + len(others)),
        out_specs=HBM,
        input_output_aliases={0: 0},
        compiler_params=PARAMS,
        cost_estimate=pl.CostEstimate(flops=flops, bytes_accessed=0, transcendentals=0),
    )(value, *others)


def tile(consts, own, other, diagonal, loss, logits, dlogit):
    scale, shift_b = jnp.exp(consts[0]), consts[1]
    logits[...] = lax.dot_general(own[...], other[...], (((1,), (1,)), ((), ())), preferred_element_type=WIDE)
    for i in range(logits.shape[0] // PIECE):
        rows = pl.ds(i * PIECE, PIECE)
        value = scale * logits[rows] + shift_b
        if diagonal:
            shape = value.shape
            same = lax.broadcasted_iota(jnp.int32, shape, 0) + i * PIECE == lax.broadcasted_iota(jnp.int32, shape, 1)
            value = jnp.where(same, -value, value)
        small = jnp.exp(-jnp.abs(value))
        loss[rows] += jnp.sum(jnp.maximum(value, 0.0) + jnp.log(1.0 + small), axis=-1, keepdims=True)
        grad = jnp.where(value >= 0, scale, scale * small) * pl.reciprocal(1.0 + small)
        if diagonal:
            grad = jnp.where(same, -grad, grad)
        dlogit[rows] = grad.astype(HALF)


def add_grad(grad, dlogit, other, fresh=False, base=None):
    for i in range(grad.shape[1] // LANES):
        cols = pl.ds(i * LANES, LANES)
        part = jnp.dot(dlogit[...], other[:, cols], preferred_element_type=WIDE)
        grad[:, cols] = part if fresh else (grad if base is None else base)[:, cols] + part


def first_kernel(consts, u, v, grad_u, grad_v, loss_u, loss_v, logits, dlogit):
    loss_u[...] = jnp.zeros_like(loss_u)
    loss_v[...] = jnp.zeros_like(loss_v)
    for own, grad, loss, others in ((u, grad_u, loss_u, (v,)), (v, grad_v, loss_v, (u,))):
        for i, other in enumerate(others):
            tile(consts, own, other, i == 0, loss, logits, dlogit)
            add_grad(grad, dlogit, other, i == 0)


def back(rows, values, norm, grad):
    inverse = 1.0 / norm[rows]
    value = grad[rows]
    along = jnp.sum(values * value, axis=-1, keepdims=True) * (inverse * inverse)
    return (value - values * along) * inverse


def second_kernel(consts, u, v, beside, across, passed, near, turned, images, texts, norm_v, grad_u_in, grad_v_in, loss_u_in,
                  loss_v_in, grad_u, grad_v, loss_u, loss_v, logits, dlogit, block, wide, sems):
    core, y = rows_place()
    fetch(core == 0, images, texts, wide, sems, True)
    loss_u[...] = loss_u_in[...]
    loss_v[...] = loss_v_in[...]
    tile(consts, u, across, False, loss_u, logits, dlogit)
    add_grad(grad_u, dlogit, across, base=grad_u_in)
    tile(consts, v, beside, False, loss_v, logits, dlogit)
    add_grad(grad_v, dlogit, beside, base=grad_v_in)
    tile(consts, v, passed, False, loss_v, logits, dlogit)
    add_grad(grad_v, dlogit, passed)
    block[...] = jnp.where(y == jnp.where(core == 0, 7, 0), turned[...], near[...])
    tile(consts, v, block, False, loss_v, logits, dlogit)
    add_grad(grad_v, dlogit, block)
    for i in range(wide.shape[0] // PIECE):
        rows = arrived(i, images, wide, sems)
        grad_v[rows] = back(rows, wide[rows], norm_v, grad_v)


def last_kernel(consts, u, passed, passed_turned, far, leap, far_turned, images, texts, norm_u, grad_u_in, grad_v, loss_u_in,
                loss_v, row_loss, image_grad, text_grad, grad_u, loss_u, logits, dlogit, block, wide, sems, out_sems, v_sem):
    core, y = rows_place()
    count = wide.shape[0]
    pieces = count // PIECE
    fetch(core == 0, images, texts, wide, sems, False)

    @pl.when(core == 0)
    def _():
        pltpu.make_async_copy(grad_v, text_grad, v_sem).start()

    @pl.when(core != 0)
    def _():
        pltpu.make_async_copy(grad_v, image_grad, v_sem).start()

    edge, after = jnp.where(core == 0, 0, 7), jnp.where(core == 0, 1, 6)
    loss_u[...] = loss_u_in[...]
    block[...] = jnp.where(y == edge, passed_turned[...], passed[...])
    tile(consts, u, block, False, loss_u, logits, dlogit)
    add_grad(grad_u, dlogit, block, base=grad_u_in)
    block[...] = jnp.where(y == edge, leap[...], jnp.where(y == after, far_turned[...], far[...]))
    tile(consts, u, block, False, loss_u, logits, dlogit)
    add_grad(grad_u, dlogit, block)
    for i in range(pieces):
        rows = arrived(i, images, wide, sems)
        grad_u[rows] = back(rows, wide[rows], norm_u, grad_u)

        @pl.when(core == 0)
        def _():
            pltpu.make_async_copy(grad_u.at[rows], image_grad.at[rows], out_sems.at[i]).start()

        @pl.when(core != 0)
        def _():
            pltpu.make_async_copy(grad_u.at[rows], text_grad.at[rows], out_sems.at[i]).start()

    total = jnp.where(core == 0, loss_u[...], loss_v[...]) / (BAND * count)
    row_loss[...] = jnp.broadcast_to(total, (count, 128)).T[0:1]
    for i in range(pieces):
        rows = pl.ds(i * PIECE, PIECE)
        pltpu.make_async_copy(grad_u.at[rows], image_grad.at[rows], out_sems.at[i]).wait()
    pltpu.make_async_copy(grad_v, text_grad, v_sem).wait()


VMEM = pl.BlockSpec(memory_space=pltpu.VMEM)
SMEM = pl.BlockSpec(memory_space=pltpu.SMEM)
HBM = pl.BlockSpec(memory_space=pl.ANY)
PARAMS = pltpu.CompilerParams(vmem_limit_bytes=24 * 2**20)


def cost(tiles):
    return pl.CostEstimate(flops=int(tiles * 40) * 256 * 256 * 1152, bytes_accessed=4 * 2**20, transcendentals=0)


def local(images, texts, log_temp, bias):
    pairs = routes()
    count, width = images.shape
    pieces = count // PIECE
    consts = jnp.concatenate([log_temp, bias])
    half = jax.ShapeDtypeStruct((count, width), HALF)
    wide = jax.ShapeDtypeStruct((count, width), WIDE)
    column = jax.ShapeDtypeStruct((count, 1), WIDE)
    logits = pltpu.VMEM((count, count), WIDE)
    dlogit = pltpu.VMEM((count, count), HALF)
    half_room = pltpu.VMEM((count, width), HALF)
    wide_room = pltpu.VMEM((count, width), WIDE)
    column_room = pltpu.VMEM((count, 1), WIDE)
    sems = pltpu.SemaphoreType.DMA((pieces,))

    def unit(swap, room):
        return pl.pallas_call(
            functools.partial(unit_kernel, swap),
            out_shape=(half, column),
            in_specs=[HBM, HBM],
            out_specs=(VMEM, VMEM),
            scratch_shapes=[wide_room, sems],
            compiler_params=pltpu.CompilerParams(vmem_limit_bytes=room * 2**20),
        )(images, texts)

    u, norm_u = unit(False, 24)
    near = send(u, pairs["near"])
    v, norm_v = unit(True, 24)
    across = send(v, pairs["across"])
    turned = send(near, pairs["turned"])
    leap = send(u, pairs["leap"])
    beside = send(after(v, near), pairs["swap"])
    far = send(near, pairs["far"])
    passed_near = send(near, pairs["pass_near"])
    grad_u, grad_v, loss_u, loss_v = pl.pallas_call(
        first_kernel,
        out_shape=(wide, wide, column, column),
        in_specs=[SMEM] + [VMEM] * 2,
        out_specs=(VMEM,) * 4,
        scratch_shapes=[logits, dlogit],
        compiler_params=PARAMS,
        cost_estimate=cost(0.1),
    )(consts, u, v)
    across = after(across, leap, loss_u)
    passed_across = send(across, pairs["swap"])
    turned = after(turned, flops=35 * 10**8)
    turned = after(turned, far, passed_near, beside)
    far_turned = after(send(turned, pairs["far_turned"]), flops=2 * 10**9)
    passed_turned = send(turned, pairs["pass_turned"])
    grad_u, grad_v, loss_u, loss_v = pl.pallas_call(
        second_kernel,
        out_shape=(wide, wide, column, column),
        in_specs=[SMEM] + [VMEM] * 7 + [HBM] * 2 + [VMEM] * 5,
        out_specs=(VMEM,) * 4,
        scratch_shapes=[logits, dlogit, half_room, wide_room, sems],
        compiler_params=PARAMS,
        cost_estimate=cost(3),
    )(consts, u, v, beside, across, passed_across, near, turned, images, texts, norm_v, grad_u, grad_v, loss_u, loss_v)
    row_loss, image_grad, text_grad = pl.pallas_call(
        last_kernel,
        out_shape=(jax.ShapeDtypeStruct((1, count), WIDE), wide, wide),
        in_specs=[SMEM] + [VMEM] * 6 + [HBM] * 2 + [VMEM] * 5,
        out_specs=(VMEM, HBM, HBM),
        scratch_shapes=[wide_room, column_room, logits, dlogit, half_room, wide_room, sems, sems, pltpu.SemaphoreType.DMA],
        compiler_params=PARAMS,
        cost_estimate=cost(2),
    )(consts, u, passed_near, passed_turned, far, leap, far_turned, images, texts, norm_u, grad_u, grad_v, loss_u, loss_v)
    return (row_loss.reshape(count), image_grad, text_grad)


def solution(mesh):
    placed = (P(AXES, None), P(AXES, None), P(), P())
    return jax.shard_map(
        local,
        mesh=mesh,
        in_specs=placed,
        out_specs=(P(AXES), P(AXES, None), P(AXES, None)),
        check_vma=False,
    )
```
